256 devices in a mesh: phase: 8 (over z), tensor: 32 (over x, y, core).
Axes of the slice: x: 4, y: 4, z: 8, core: 2. Of those that a mesh axis runs over, the one named last changes fastest.
Arguments:
- incoming: bfloat16 [8, 2048, 1536], P('phase'), may hold values from -6 to 6
- fresh_grad: bfloat16 [2048, 1536], P('tensor'), may hold values from -6 to 6
- pre_act: bfloat16 [2, 8, 2048, 12288], P(None, 'phase', None, 'tensor'), may hold values from -6 to 6
- conv_pre: bfloat16 [2, 8, 2048, 1536], P(None, 'phase', 'tensor'), may hold values from -6 to 6
- w_in: bfloat16 [8, 1536, 12288], P('phase', None, 'tensor'), may hold values from -0.15625 to 0.15625
- w_out: bfloat16 [8, 12288, 1536], P('phase', 'tensor'), may hold values from -0.0546875 to 0.0546875
- pw_out: bfloat16 [8, 1536, 1536], P('phase', 'tensor'), may hold values from -0.15625 to 0.15625
- kernel: float32 [8, 31, 1536], P('phase'), may hold values from -1 to 1
Outputs:
- input_grads: bfloat16 [2, 8, 2048, 1536], P(None, 'phase', 'tensor')
The draws below stay inside these ranges and needn't reach their ends.
All inputs are finite; a program needn't handle non-finite values.
Results may differ from the reference program's by a relative error of at most 0.023.
Values may be sent and summed in bfloat16 or wider, within the bound.
No kernel may reach another device: no remote copies, remote signals or barrier semaphores. Data moves between devices by JAX's collectives and lax.ppermute only.
A program may use at most 128 MiB of HBM per device.

```python
import jax
import jax.numpy as jnp
from jax import lax

D = 1536
FF = 12288
TAPS = 31
STEPS = 2
PHASES = 8
FRAMES = 2048
N_TENSOR = 32


def levels(own_key, dims, split, least, largest):
    factor_of, own = 1.0, jax.random.fold_in(own_key, 6)
    for axis_at, parts in split:
        steps = jnp.exp(jax.random.uniform(jax.random.fold_in(own, axis_at), (parts,), jnp.float32, least / len(split), largest / len(split)))
        factor_of = factor_of * jnp.repeat(steps, dims[axis_at] // parts).reshape([-1 if axis == axis_at else 1 for axis in range(len(dims))])
    return factor_of


def scatter_about(stream_key, extent, width, most, cuts=(), dtype=jnp.bfloat16):
    result = width * jax.random.normal(stream_key, extent, jnp.float32)
    if cuts:
        result = result * levels(stream_key, extent, cuts, -0.22, 0.18)
    return jnp.clip(result, -most, most).astype(dtype)


def setup_inputs(seed: int = 0) -> dict:
    arg_keys = jax.random.split(jax.random.key(seed), 9)
    return {
        "incoming": scatter_about(arg_keys[0], (PHASES, FRAMES, D), 1.0, 6.0, ((0, 8),)),
        "fresh_grad": scatter_about(arg_keys[1], (FRAMES, D), 1.0, 6.0, ((0, 32),)),
        "pre_act": scatter_about(arg_keys[2], (STEPS, PHASES, FRAMES, FF), 1.5, 6.0, ((1, 8), (3, 32))),
        "conv_pre": scatter_about(arg_keys[3], (STEPS, PHASES, FRAMES, D), 1.5, 6.0, ((1, 8), (2, 32))),
        "w_in": scatter_about(arg_keys[4], (PHASES, D, FF), D ** -0.5, 0.15625, ((0, 8), (2, 32))),
        "w_out": scatter_about(arg_keys[5], (PHASES, FF, D), FF ** -0.5, 0.0546875, ((0, 8), (1, 32))),
        "pw_out": scatter_about(arg_keys[6], (PHASES, D, D), D ** -0.5, 0.15625, ((0, 8), (1, 32))),
        "kernel": scatter_about(arg_keys[7], (PHASES, TAPS, D), TAPS ** -0.5, 1.0, ((0, 8),), jnp.float32),
    }


def gated_back(hidden_grad, activation):
    pre_value = activation.astype(jnp.float32)
    sigmoid_a = jax.nn.sigmoid(pre_value)
    return (hidden_grad * sigmoid_a * (1.0 + pre_value * (1.0 - sigmoid_a))).astype(jnp.bfloat16)


def summed_terms(gate_grad, first_proj):
    block_width = FF // N_TENSOR

    def add_block(block_index, total):
        start = (block_index * block_width).astype(jnp.int32)
        grad_cols = lax.dynamic_slice_in_dim(gate_grad, start, block_width, 1)
        proj_cols = lax.dynamic_slice_in_dim(first_proj, start, block_width, 1)
        partial_sum = jnp.dot(grad_cols, proj_cols.T, preferred_element_type=jnp.float32).astype(jnp.bfloat16)
        partial_sum = lax.optimization_barrier(partial_sum)
        return total + partial_sum.astype(jnp.float32)

    return lax.fori_loop(0, N_TENSOR, add_block, jnp.zeros((FRAMES, D), jnp.float32))


def phase_back(gradient, activation, conv_in, first_proj, second_proj, point_out, taps_here):
    hidden_grad = jnp.dot(gradient, second_proj.T, preferred_element_type=jnp.float32)
    gate_grad = gated_back(hidden_grad, activation)
    summed = summed_terms(gate_grad, first_proj)
    residual = (gradient.astype(jnp.float32) + summed).astype(jnp.bfloat16)
    swish_grad = jnp.dot(residual, point_out.T, preferred_element_type=jnp.float32).astype(jnp.bfloat16)
    conv_grad = gated_back(swish_grad.astype(jnp.float32), conv_in)
    reach_half = (TAPS - 1) // 2
    padded = jnp.pad(conv_grad, ((reach_half, reach_half), (0, 0)))
    running = jnp.zeros((FRAMES, D), jnp.float32)
    for tap_index in range(TAPS):
        offset_row = TAPS - 1 - tap_index
        running = running + taps_here[tap_index].astype(jnp.float32) * padded[offset_row:offset_row + FRAMES].astype(jnp.float32)
    return (residual.astype(jnp.float32) + running).astype(jnp.bfloat16)


def reference(incoming, fresh_grad, pre_act, conv_pre, w_in, w_out, pw_out, kernel):
    first_turn = []
    for phase_index in range(PHASES):
        first_turn.append(phase_back(incoming[phase_index], pre_act[0, phase_index], conv_pre[0, phase_index], w_in[phase_index], w_out[phase_index], pw_out[phase_index], kernel[phase_index]))
    second_turn = []
    for phase_index in range(PHASES):
        if phase_index + 1 < PHASES:
            arriving = first_turn[phase_index + 1]
        else:
            arriving = fresh_grad
        second_turn.append(phase_back(arriving, pre_act[1, phase_index], conv_pre[1, phase_index], w_in[phase_index], w_out[phase_index], pw_out[phase_index], kernel[phase_index]))
    return jnp.stack([jnp.stack(first_turn), jnp.stack(second_turn)])
```

```python
import functools

import jax
import jax.numpy as jnp
from jax import lax
from jax.experimental import pallas as pl
from jax.experimental.pallas import tpu as pltpu
from jax.sharding import PartitionSpec as P

NX, NY, NC = 4, 4, 2
ROWS = 32
TILE = 128
BF16, F32 = jnp.bfloat16, jnp.float32


def place(x, y, c):
    return (x % NX * NY + y % NY) * NC + c


def route(dx, dy):
    return [
        (place(x, y, c), place(x + dx, y + dy, c))
        for x in range(NX)
        for y in range(NY)
        for c in range(NC)
    ]


def to_x(value, d):
    return lax.ppermute(value, "tensor", route(d, 0))


def to_y(value, d):
    return lax.ppermute(value, "tensor", route(0, d))


def swap_cores(value):
    return lax.ppermute(
        value,
        "tensor",
        [(place(x, y, c), place(x, y, 1 - c)) for x in range(NX) for y in range(NY) for c in range(NC)],
    )


def gated_back(hidden_grad, activation):
    pre_value = activation.astype(F32)
    sigmoid_a = jax.nn.sigmoid(pre_value)
    return (hidden_grad * sigmoid_a * (1.0 + pre_value * (1.0 - sigmoid_a))).astype(BF16)


def times_transpose(left, right):
    return lax.dot_general(left, right, (((1,), (1,)), ((), ())), preferred_element_type=F32)


def ff_body(steps, grads, *refs):
    place_ref, refs = refs[0], refs[1:]
    g_refs, refs = refs[:grads], refs[grads:]
    own_refs, refs = refs[:8], refs[8:]
    other_refs, refs = refs[:8], refs[8:]
    out_own, out_other, in_own, in_other, a_ref, b_ref, total = refs
    step = pl.program_id(0)
    gradient = jnp.concatenate([r[...].reshape(-1, r.shape[-1]) for r in g_refs], axis=0)
    second = jnp.concatenate([out_own[...], out_other[...]], axis=0)
    hidden = times_transpose(gradient, second)
    pre = jnp.concatenate(
        [
            jnp.concatenate([r[...] for r in own_refs], axis=0),
            jnp.concatenate([r[...] for r in other_refs], axis=0),
        ],
        axis=1,
    )
    gate = gated_back(hidden, pre)
    first = jnp.concatenate([in_own[...], in_other[...]], axis=1)
    partial = times_transpose(gate, first)

    @pl.when(step == 0)
    def _():
        total[...] = partial

    @pl.when((step > 0) & (step < steps - 1))
    def _():
        total[...] += partial

    @pl.when(step == steps - 1)
    def _():
        done = (total[...] + partial).astype(BF16)
        half = done.shape[0] // 2
        a_ref[...] = done[:half].reshape(a_ref.shape)
        b_ref[...] = done[half:].reshape(b_ref.shape)


def ff_back(here, d, turn, grads, own_pre, other_pre, second_own, second_other, first_own, first_other):
    width = second_own.shape[1]
    steps = second_own.shape[0] // TILE

    def spots(ref):
        x, y, c = ref[0], ref[1], ref[2]
        a = [((x + k) % NX, (y + d) % NY, c, 0) for k in range(NX)]
        b = [((x + d) % NX, (y + k) % NY, c, 1) for k in range(NY)]
        return a + b

    if len(grads) == 1:
        grad_args = [grads[0]] * 8
        grad_specs = [
            pl.BlockSpec((None, None, None, None, ROWS, width), lambda j, ref, i=i: (*spots(ref)[i], 0, 0))
            for i in range(8)
        ]
    else:
        grad_args = list(grads)
        grad_specs = [pl.BlockSpec(g.shape, lambda j, ref: (0, 0, 0)) for g in grads]
    own_specs = [
        pl.BlockSpec(
            (None, None, None, None, None, ROWS, TILE), lambda j, ref, i=i: (turn, *spots(ref)[i], 0, j)
        )
        for i in range(8)
    ]

    def other_spot(j, ref, i):
        x, y, _, h = spots(ref)[i]
        return (x, y, h, 0, j)

    other_specs = [
        pl.BlockSpec((None, None, None, ROWS, TILE), functools.partial(other_spot, i=i)) for i in range(8)
    ]
    second_spec = pl.BlockSpec((TILE, width), lambda j, ref: (j, 0))
    first_spec = pl.BlockSpec((width, TILE), lambda j, ref: (0, j))
    out = jax.ShapeDtypeStruct((4, ROWS, width), BF16)
    out_spec = pl.BlockSpec((4, ROWS, width), lambda j, ref: (0, 0, 0))
    units = 2 * TILE * steps
    return pl.pallas_call(
        functools.partial(ff_body, steps, len(grad_args)),
        grid_spec=pltpu.PrefetchScalarGridSpec(
            num_scalar_prefetch=1,
            grid=(steps,),
            in_specs=grad_specs + own_specs + other_specs + [second_spec] * 2 + [first_spec] * 2,
            out_specs=[out_spec, out_spec],
            scratch_shapes=[pltpu.VMEM((8 * ROWS, width), F32)],
        ),
        out_shape=[out, out],
        compiler_params=pltpu.CompilerParams(vmem_limit_bytes=32 * 1024 * 1024),
        cost_estimate=pl.CostEstimate(
            flops=4 * 8 * ROWS * width * units,
            bytes_accessed=4 * units * width + 4 * 8 * ROWS * width,
            transcendentals=8 * ROWS * units,
        ),
        name="ff_back",
    )(here, *grad_args, *([own_pre] * 8), *([other_pre] * 8), second_own, second_other, first_own, first_other)


def turned(stacked, by, count):
    doubled = jnp.concatenate([stacked, stacked], axis=0)
    return lax.dynamic_slice_in_dim(doubled, (count - by) % count, count, 0)


def gather_point(point, x, y, c):
    half = point.shape[1] // 2
    left, right = point[:, :half], point[:, half:]
    left = jnp.stack([left] + [to_x(left, -d) for d in range(1, NX)])
    right = jnp.stack([right] + [to_y(right, -d) for d in range(1, NY)])
    left = turned(left, x, NX)
    right = turned(right, y, NY)
    left = turned(jnp.stack([left] + [to_y(left, -d) for d in range(1, NY)]), y, NY)
    right = turned(jnp.stack([right] + [to_x(right, -d) for d in range(1, NX)]), x, NX)
    both = jnp.concatenate([left.transpose(1, 0, 2, 3), right], axis=3)
    other = swap_cores(both)
    full = jnp.where(c == 0, jnp.stack([both, other], axis=2), jnp.stack([other, both], axis=2))
    return full.reshape(-1, point.shape[1])


def extended(block, width):
    count = lax.axis_size("tensor")
    forward = [(i, i + 1) for i in range(count - 1)]
    backward = [(target, source) for source, target in forward]
    low = lax.ppermute(block[-width:], "tensor", forward)
    high = lax.ppermute(block[:width], "tensor", backward)
    return jnp.concatenate([low, block, high], axis=0)


def scattered(parts_a, parts_b, own):
    own = own.astype(F32)
    a = [parts_a[0]] + [to_y(parts_a[d], d) for d in range(1, NY)]
    b = [parts_b[0]] + [to_x(parts_b[d], d) for d in range(1, NX)]
    sum_a = sum(v.astype(F32) for v in a)
    sum_b = sum(v.astype(F32) for v in b)
    send_a, send_b = sum_a.astype(BF16), sum_b.astype(BF16)
    a = [sum_a[0]] + [to_x(send_a[d], d).astype(F32) for d in range(1, NX)]
    b = [sum_b[0]] + [to_y(send_b[d], d).astype(F32) for d in range(1, NY)]
    return jnp.concatenate([own[:ROWS] + sum(a), own[ROWS:] + sum(b)], axis=0).astype(BF16)


def phase_tail(residual, conv_in, point_full, taps_here):
    swish_grad = times_transpose(residual, point_full).astype(BF16)
    conv_grad = gated_back(swish_grad.astype(F32), conv_in)
    taps_total, row_count = taps_here.shape[0], residual.shape[0]
    padded = extended(conv_grad, (taps_total - 1) // 2)
    running = jnp.zeros(residual.shape, F32)
    for tap_index in range(taps_total):
        offset_row = taps_total - 1 - tap_index
        running = running + taps_here[tap_index] * padded[offset_row : offset_row + row_count].astype(F32)
    return (residual.astype(F32) + running).astype(BF16)


def per_device(incoming, fresh_grad, pre_act, conv_pre, w_in, w_out, pw_out, kernel):
    first_proj, second_proj, taps_here = w_in[0], w_out[0], kernel[0]
    spot = lax.axis_index("tensor")
    x, y, c = spot // (NY * NC), spot // NC % NY, spot % NC
    here = jnp.stack([x, y, c]).astype(jnp.int32)
    units, width = second_proj.shape

    second_other = swap_cores(second_proj)
    first_other = swap_cores(first_proj)
    own_pre = pre_act.reshape(2, NX, NY, NC, 2, ROWS, units)
    given = lax.dynamic_index_in_dim(own_pre, 1 - c, 3, keepdims=False)
    other_pre = [swap_cores(given[0]), swap_cores(given[1])]
    weights = (second_proj, second_other, first_proj, first_other)
    point_full = gather_point(pw_out[0], x, y, c)

    whole = incoming.reshape(NX, NY, NC, 2, ROWS, width)
    parts = [ff_back(here, d, 0, [whole], own_pre, other_pre[0], *weights) for d in range(4)]
    own_first = lax.dynamic_slice_in_dim(incoming[0], spot * 2 * ROWS, 2 * ROWS, 0)
    residual = scattered([p[0] for p in parts], [p[1] for p in parts], own_first)
    first_turn = phase_tail(residual, conv_pre[0, 0], point_full, taps_here)

    phases = lax.axis_size("phase")
    received = lax.ppermute(first_turn, "phase", [(i, i - 1) for i in range(1, phases)])
    arriving = jnp.where(lax.axis_index("phase") == phases - 1, fresh_grad, received)
    lower, upper = arriving[:ROWS], arriving[ROWS:]
    near_a = jnp.stack([lower] + [to_x(lower, -d) for d in range(1, NX)])
    near_b = jnp.stack([upper] + [to_y(upper, -d) for d in range(1, NY)])
    far_a = [near_a] + [to_y(near_a, -d) for d in range(1, NY)]
    far_b = [near_b] + [to_x(near_b, -d) for d in range(1, NX)]
    parts = [
        ff_back(here, d, 1, [far_a[d], far_b[d]], own_pre, other_pre[1], *weights) for d in range(4)
    ]
    residual = scattered([p[0] for p in parts], [p[1] for p in parts], arriving)
    second_turn = phase_tail(residual, conv_pre[1, 0], point_full, taps_here)
    return jnp.stack([first_turn, second_turn])[:, None]


def solution(mesh):
    return jax.shard_map(
        per_device,
        mesh=mesh,
        in_specs=(
            P("phase", None, None),
            P("tensor", None),
            P(None, "phase", None, "tensor"),
            P(None, "phase", "tensor", None),
            P("phase", None, "tensor"),
            P("phase", "tensor", None),
            P("phase", "tensor", None),
            P("phase", None, None),
        ),
        out_specs=P(None, "phase", "tensor", None),
        check_vma=False,
    )
```

```python
import functools

import jax
import jax.numpy as jnp
from jax import lax
from jax.experimental import pallas as pl
from jax.experimental.pallas import tpu as pltpu
from jax.sharding import PartitionSpec as P

NX, NY, NC = 4, 4, 2
ROWS = 32
BF16, F32 = jnp.bfloat16, jnp.float32
CHIPS = [(x, y, c) for x in range(NX) for y in range(NY) for c in range(NC)]


def place(x, y, c):
    return (x % NX * NY + y % NY) * NC + c


def to_x(value, d):
    return lax.ppermute(value, "tensor", [(place(x, y, c), place(x + d, y, c)) for x, y, c in CHIPS])


def to_y(value, d):
    return lax.ppermute(value, "tensor", [(place(x, y, c), place(x, y + d, c)) for x, y, c in CHIPS])


def swap_cores(value):
    return lax.ppermute(value, "tensor", [(place(x, y, c), place(x, y, 1 - c)) for x, y, c in CHIPS])


def after(value, *others):
    return lax.optimization_barrier((value, *others))[0]


def gated_back(hidden_grad, activation):
    pre_value = activation.astype(F32)
    sigmoid_a = jax.nn.sigmoid(pre_value)
    return (hidden_grad * sigmoid_a * (1.0 + pre_value * (1.0 - sigmoid_a))).astype(BF16)


def times_transpose(left, right):
    return lax.dot_general(left, right, (((1,), (1,)), ((), ())), preferred_element_type=F32)


def ff_body(turn, dists, whole, place_ref, own_pre, other_pre, out_own, out_other, in_own, in_other, *refs):
    results, g_refs = refs[-2 * len(dists) :], refs[: -2 * len(dists)]
    x, y, c = place_ref[0], place_ref[1], place_ref[2]
    spots = []
    for d in dists:
        spots += [((x + k) % NX, (y + d) % NY, 0) for k in range(NX)]
        spots += [((x + d) % NX, (y + k) % NY, 1) for k in range(NY)]
    if whole:
        blocks = [g_refs[0][i, j, c, h] for i, j, h in spots]
    else:
        blocks = [r[...].reshape(-1, r.shape[-1]) for r in g_refs]
    gradient = jnp.concatenate(blocks, axis=0)
    gates = []
    for second, pre in (
        (out_own, [own_pre[turn, i, j, c, h] for i, j, h in spots]),
        (out_other, [other_pre[i, j, h] for i, j, h in spots]),
    ):
        hidden = times_transpose(gradient, second[...])
        gates.append(gated_back(hidden, jnp.concatenate(pre, axis=0)))
    first = jnp.concatenate([in_own[...], in_other[...]], axis=1)
    partial = times_transpose(jnp.concatenate(gates, axis=1), first).astype(BF16)
    for i, result in enumerate(results):
        result[...] = partial[i * 4 * ROWS : (i + 1) * 4 * ROWS].reshape(result.shape)


def ff_back(here, turn, dists, grads, own_pre, other_pre, weights):
    units, width = weights[0].shape
    whole = grads[0].ndim == 6
    rows = 8 * ROWS * len(dists)
    operands = [own_pre, other_pre, *weights, *grads]
    operands = [pltpu.with_memory_space_constraint(v, pltpu.VMEM) for v in operands]
    inside = pl.BlockSpec(memory_space=pltpu.VMEM)
    return pl.pallas_call(
        functools.partial(ff_body, turn, dists, whole),
        in_specs=[pl.BlockSpec(memory_space=pltpu.SMEM)] + [inside] * len(operands),
        out_specs=[inside] * (2 * len(dists)),
        out_shape=[jax.ShapeDtypeStruct((4, ROWS, width), BF16)] * (2 * len(dists)),
        compiler_params=pltpu.CompilerParams(vmem_limit_bytes=24 * 1024 * 1024),
        cost_estimate=pl.CostEstimate(
            flops=8 * rows * width * units,
            bytes_accessed=8 * units * width + 4 * rows * width,
            transcendentals=2 * rows * units,
        ),
        name="ff_back",
    )(here, *operands)


def ring(near, send, *awaited):
    following, previous = send(near, -1), send(near, 1)
    half = near.shape[0] // 2
    if awaited:
        following, previous = after(following, *awaited), after(previous, *awaited)
    return near, following, (send(following[:half], -1), send(previous[half:], 1)), previous


def extended(block, width):
    count = lax.axis_size("tensor")
    forward = [(i, i + 1) for i in range(count - 1)]
    backward = [(target, source) for source, target in forward]
    low = lax.ppermute(block[-width:], "tensor", forward)
    high = lax.ppermute(block[:width], "tensor", backward)
    return jnp.concatenate([low, block, high], axis=0)


def scattered(parts_a, parts_b, own):
    own = own.astype(F32)
    a = [parts_a[0]] + [to_y(parts_a[d], d) for d in range(1, NY)]
    b = [parts_b[0]] + [to_x(parts_b[d], d) for d in range(1, NX)]
    sum_a = sum(v.astype(F32) for v in a)
    sum_b = sum(v.astype(F32) for v in b)
    send_a, send_b = sum_a.astype(BF16), sum_b.astype(BF16)
    a = [sum_a[0]] + [to_x(send_a[d], d).astype(F32) for d in range(1, NX)]
    b = [sum_b[0]] + [to_y(send_b[d], d).astype(F32) for d in range(1, NY)]
    return jnp.concatenate([own[:ROWS] + sum(a), own[ROWS:] + sum(b)], axis=0).astype(BF16)


def phase_tail(residual, conv_in, point_full, taps_here):
    swish_grad = times_transpose(residual, point_full).astype(BF16)
    conv_grad = gated_back(swish_grad.astype(F32), conv_in)
    taps_total, row_count = taps_here.shape[0], residual.shape[0]
    padded = extended(conv_grad, (taps_total - 1) // 2)
    running = jnp.zeros(residual.shape, F32)
    for tap_index in range(taps_total):
        offset_row = taps_total - 1 - tap_index
        running = running + taps_here[tap_index] * padded[offset_row : offset_row + row_count].astype(F32)
    return (residual.astype(F32) + running).astype(BF16)


def per_device(incoming, fresh_grad, pre_act, conv_pre, w_in, w_out, pw_out, kernel):
    first_proj, second_proj, taps_here = w_in[0], w_out[0], kernel[0]
    spot = lax.axis_index("tensor")
    x, y, c = spot // (NY * NC), spot // NC % NY, spot % NC
    here = jnp.stack([x, y, c]).astype(jnp.int32)
    units, width = second_proj.shape

    own_pre = pre_act.reshape(2, NX, NY, NC, 2, ROWS, units)
    second_other = swap_cores(second_proj)
    first_other = swap_cores(first_proj)
    given = lax.dynamic_index_in_dim(own_pre[0], 1 - c, 2, keepdims=False)
    other_pre = swap_cores(given)
    weights = (second_proj, second_other, first_proj, first_other)

    whole = incoming.reshape(NX, NY, NC, 2, ROWS, width)
    a2, b2 = ff_back(here, 0, (2,), [whole], own_pre, other_pre, weights)
    a1, b1, a3, b3 = ff_back(after(here, a2), 0, (1, 3), [whole], own_pre, other_pre, weights)
    a0, b0 = ff_back(after(here, a1), 0, (0,), [whole], own_pre, other_pre, weights)
    own_first = lax.dynamic_slice_in_dim(incoming[0], spot * 2 * ROWS, 2 * ROWS, 0)
    point_full = lax.all_gather(pw_out[0], "tensor", axis=0, tiled=True)
    residual = scattered((a0, a1, a2, a3), (b0, b1, b2, b3), own_first)
    first_turn = phase_tail(residual, conv_pre[0, 0], point_full, taps_here)

    given = lax.dynamic_index_in_dim(after(own_pre, a0)[1], 1 - c, 2, keepdims=False)
    other_pre = swap_cores(given)
    phases = lax.axis_size("phase")
    received = lax.ppermute(first_turn, "phase", [(i, i - 1) for i in range(1, phases)])
    arriving = jnp.where(lax.axis_index("phase") == phases - 1, fresh_grad, received)
    lower, upper = arriving[:ROWS], arriving[ROWS:]
    near_a = jnp.stack([lower] + [to_x(lower, -d) for d in range(1, NX)])
    near_b = jnp.stack([upper] + [to_y(upper, -d) for d in range(1, NY)])
    far_a, far_b = ring(near_a, to_y), ring(near_b, to_x)
    rest = (own_pre, other_pre, weights)
    a0, b0 = ff_back(here, 1, (0,), [near_a, near_b], *rest)
    a1, b1, a3, b3 = ff_back(after(here, a0), 1, (1, 3), [far_a[1], far_b[1], far_a[3], far_b[3]], *rest)
    a2, b2 = ff_back(after(here, a1), 1, (2,), [*far_a[2], *far_b[2]], *rest)
    residual = scattered((a0, a1, a2, a3), (b0, b1, b2, b3), arriving)
    second_turn = phase_tail(residual, conv_pre[1, 0], point_full, taps_here)
    return jnp.stack([first_turn, second_turn])[:, None]


def solution(mesh):
    return jax.shard_map(
        per_device,
        mesh=mesh,
        in_specs=(
            P("phase", None, None),
            P("tensor", None),
            P(None, "phase", None, "tensor"),
            P(None, "phase", "tensor", None),
            P("phase", None, "tensor"),
            P("phase", "tensor", None),
            P("phase", "tensor", None),
            P("phase", None, None),
        ),
        out_specs=P(None, "phase", "tensor", None),
        check_vma=False,
    )
```

```python
import functools

import jax
import jax.numpy as jnp
from jax import lax
from jax.experimental import pallas as pl
from jax.experimental.pallas import tpu as pltpu
from jax.sharding import PartitionSpec as P

NX, NY, NC = 4, 4, 2
SIDE, ROWS, EDGE = 4, 64, 16
BF16, F32 = jnp.bfloat16, jnp.float32
CHIPS = [(x, y, c) for x in range(NX) for y in range(NY) for c in range(NC)]


def place(x, y, c):
    return (x % NX * NY + y % NY) * NC + c


def along(value, d, first):
    pairs = []
    for x, y, c in CHIPS:
        dx, dy = (0, d) if (c == 0) == first else (d, 0)
        pairs.append((place(x, y, c), place(x + dx, y + dy, c)))
    return lax.ppermute(value, "tensor", pairs)


def swap_cores(value):
    return lax.ppermute(value, "tensor", [(place(x, y, c), place(x, y, 1 - c)) for x, y, c in CHIPS])


def after(value, *others):
    return lax.optimization_barrier((value, *others))[0]


def gated_back(hidden_grad, activation):
    pre_value = activation.astype(F32)
    sigmoid_a = jax.nn.sigmoid(pre_value)
    return (hidden_grad * sigmoid_a * (1.0 + pre_value * (1.0 - sigmoid_a))).astype(BF16)


def times_transpose(left, right):
    return lax.dot_general(left, right, (((1,), (1,)), ((), ())), preferred_element_type=F32)


def spots(place_ref, d):
    x, y, c = place_ref[0], place_ref[1], place_ref[2]
    found = []
    for k in range(SIDE):
        dx, dy = jnp.where(c == 0, k, d), jnp.where(c == 0, d, k)
        found.append(((x + dx) % NX, (y + dy) % NY))
    return found


def ff_rows(gradient, pre_own, pre_other, out_own, out_other, in_own, in_other):
    gates = [
        gated_back(times_transpose(gradient, second[...]), pre)
        for second, pre in ((out_own, pre_own), (out_other, pre_other))
    ]
    first = jnp.concatenate([in_own[...], in_other[...]], axis=1)
    return times_transpose(jnp.concatenate(gates, axis=1), first).astype(BF16)


def ff_first_body(place_ref, other_pre, out_other, in_other, own_pre, out_own, in_own, grads, *refs):
    results, (held_out, held_in, held_pre, held_grad, sems) = refs[:SIDE], refs[SIDE:]
    c = place_ref[2]
    copies = [
        (grads.at[:, :, c], held_grad),
        (out_own, held_out),
        (own_pre.at[0, :, :, c], held_pre),
        (in_own, held_in),
    ]
    copies = [pltpu.make_async_copy(src, dst, sems.at[i]) for i, (src, dst) in enumerate(copies)]
    for copy in copies:
        copy.start()
    for copy in copies:
        copy.wait()
    for d in (2, 1, 3, 0):
        found = spots(place_ref, d)
        rows = [jnp.concatenate([r[i, j] for i, j in found], axis=0) for r in (held_grad, held_pre, other_pre)]
        results[d][...] = ff_rows(*rows, held_out, out_other, held_in, in_other).reshape(results[d].shape)


def ff_first(here, grads, own_pre, other_pre, weights):
    units, width = weights[0].shape
    rows = SIDE * SIDE * ROWS
    near = [pltpu.with_memory_space_constraint(v, pltpu.VMEM) for v in (other_pre, weights[1], weights[3])]
    far = [pltpu.with_memory_space_constraint(v, pltpu.HBM) for v in (own_pre, weights[0], weights[2], grads)]
    return pl.pallas_call(
        ff_first_body,
        in_specs=[pl.BlockSpec(memory_space=pltpu.SMEM)]
        + [pl.BlockSpec(memory_space=pltpu.VMEM)] * 3
        + [pl.BlockSpec(memory_space=pltpu.HBM)] * 4,
        out_specs=[pl.BlockSpec(memory_space=pltpu.VMEM)] * SIDE,
        out_shape=[jax.ShapeDtypeStruct((SIDE, ROWS, width), BF16)] * SIDE,
        scratch_shapes=[
            pltpu.VMEM(weights[0].shape, BF16),
            pltpu.VMEM(weights[2].shape, BF16),
            pltpu.VMEM((NX, NY, ROWS, units), BF16),
            pltpu.VMEM((NX, NY, ROWS, width), BF16),
            pltpu.SemaphoreType.DMA((4,)),
        ],
        compiler_params=pltpu.CompilerParams(vmem_limit_bytes=32 * 1024 * 1024),
        cost_estimate=pl.CostEstimate(
            flops=8 * rows * width * units,
            bytes_accessed=8 * units * width + 4 * rows * width,
            transcendentals=2 * rows * units,
        ),
        name="ff_first",
    )(here, *near, *far)


def order_body(place_ref, mine, other, full, sems):
    x, y, c = place_ref[0], place_ref[1], place_ref[2]
    height = mine.shape[1]
    copies = []
    for source, core in ((mine, c), (other, 1 - c)):
        for a in range(SIDE):
            for b in range(SIDE):
                dx, dy = jnp.where(core == 0, b, a), jnp.where(core == 0, a, b)
                row = (((x + dx) % NX * NY + (y + dy) % NY) * NC + core) * height
                row = pl.multiple_of(row, height)
                i = len(copies)
                copies.append(
                    pltpu.make_async_copy(source.at[a * SIDE + b], full.at[pl.ds(row, height)], sems.at[i])
                )
    for copy in copies:
        copy.start()
    for copy in copies:
        copy.wait()


def ordered(here, mine, other):
    count, height, width = mine.shape
    mine, other = [pltpu.with_memory_space_constraint(v, pltpu.VMEM) for v in (mine, other)]
    inside = pl.BlockSpec(memory_space=pltpu.VMEM)
    return pl.pallas_call(
        order_body,
        in_specs=[pl.BlockSpec(memory_space=pltpu.SMEM), inside, inside],
        out_specs=inside,
        out_shape=jax.ShapeDtypeStruct((NC * count * height, width), BF16),
        scratch_shapes=[pltpu.SemaphoreType.DMA((NC * count,))],
        compiler_params=pltpu.CompilerParams(vmem_limit_bytes=16 * 1024 * 1024),
        cost_estimate=pl.CostEstimate(flops=0, bytes_accessed=4 * NC * count * height * width, transcendentals=0),
        name="order",
    )(here, mine, other)


def ff_body(turn, dists, place_ref, own_pre, other_pre, *refs):
    weights, refs = refs[:4], refs[4:]
    results, g_refs = refs[-len(dists) :], refs[: -len(dists)]
    found = [spot for d in dists for spot in spots(place_ref, d)]
    c = place_ref[2]
    gradient = jnp.concatenate([r[...].reshape(-1, r.shape[-1]) for r in g_refs], axis=0)
    pre_own = jnp.concatenate([own_pre[turn, i, j, c] for i, j in found], axis=0)
    pre_other = jnp.concatenate([other_pre[i, j] for i, j in found], axis=0)
    partial = ff_rows(gradient, pre_own, pre_other, *weights)
    size = SIDE * ROWS
    for i, result in enumerate(results):
        result[...] = partial[i * size : (i + 1) * size].reshape(result.shape)


def ff_back(here, turn, dists, grads, own_pre, other_pre, weights):
    units, width = weights[0].shape
    rows = SIDE * ROWS * len(dists)
    operands = [own_pre, other_pre, *weights, *grads]
    operands = [pltpu.with_memory_space_constraint(v, pltpu.VMEM) for v in operands]
    inside = pl.BlockSpec(memory_space=pltpu.VMEM)
    return pl.pallas_call(
        functools.partial(ff_body, turn, dists),
        in_specs=[pl.BlockSpec(memory_space=pltpu.SMEM)] + [inside] * len(operands),
        out_specs=[inside] * len(dists),
        out_shape=[jax.ShapeDtypeStruct((SIDE, ROWS, width), BF16)] * len(dists),
        compiler_params=pltpu.CompilerParams(vmem_limit_bytes=24 * 1024 * 1024),
        cost_estimate=pl.CostEstimate(
            flops=8 * rows * width * units,
            bytes_accessed=8 * units * width + 4 * rows * width,
            transcendentals=2 * rows * units,
        ),
        name="ff_back",
    )(here, *operands)


def gathered_back(near, back):
    following, previous = along(near, -1, True), along(near, 1, True)
    half = near.shape[0] // 2
    (p0,) = back((0,), [near])
    following, previous, p0 = lax.optimization_barrier((following, previous, p0))
    opposite = along(following[:half], -1, True), along(previous[half:], 1, True)
    p1, p3 = back((1, 3), [following, previous])
    *opposite, p1 = lax.optimization_barrier((*opposite, p1))
    (p2,) = back((2,), opposite)
    return p0, p1, p2, p3


def scattered(parts, own):
    got = [parts[0]] + [along(parts[d], d, True) for d in (2, 1, 3)]
    total = sum(v.astype(F32) for v in got)
    send = total.astype(BF16)
    got = [total[0]] + [along(send[d], d, False).astype(F32) for d in (2, 1, 3)]
    return (own.astype(F32) + sum(got)).astype(BF16)


def conv_gradient(residual, conv_in, point_full):
    swish_grad = times_transpose(residual, point_full).astype(BF16)
    return gated_back(swish_grad.astype(F32), conv_in)


def edges(block, behind):
    phases, count = lax.axis_size("phase"), lax.axis_size("tensor")

    def route(d):
        return [
            (s * count + t, (s - behind) * count + t + d)
            for s in range(behind, phases)
            for t in range(count)
            if 0 <= t + d < count
        ]

    axes = ("phase", "tensor")
    return lax.ppermute(block[-EDGE:], axes, route(1)), lax.ppermute(block[:EDGE], axes, route(-1))


def with_taps(residual, conv_grad, low, high, taps):
    row_count, last = residual.shape[0], taps.shape[0] - 1
    padded = jnp.concatenate([low, conv_grad, high], axis=0)
    running = jnp.zeros(residual.shape, F32)
    for tap_index in range(last + 1):
        offset_row = EDGE + last // 2 - tap_index
        running = running + taps[tap_index] * padded[offset_row : offset_row + row_count].astype(F32)
    return (residual.astype(F32) + running).astype(BF16)


def per_device(incoming, fresh_grad, pre_act, conv_pre, w_in, w_out, pw_out, kernel):
    first_proj, second_proj, taps_here = w_in[0], w_out[0], kernel[0]
    spot = lax.axis_index("tensor")
    x, y, c = spot // (NY * NC), spot // NC % NY, spot % NC
    here = jnp.stack([x, y, c]).astype(jnp.int32)
    units, width = second_proj.shape

    own_pre = pre_act.reshape(2, NX, NY, NC, ROWS, units)

    def other_half(turn, source):
        given = lax.dynamic_slice(source, (turn, 0, 0, 1 - c, 0, 0), (1, NX, NY, 1, ROWS, units))
        return swap_cores(given.reshape(NX, NY, ROWS, units))

    second_other = swap_cores(second_proj)
    first_other = swap_cores(first_proj)
    other_pre = other_half(0, own_pre)
    weights = (second_proj, second_other, first_proj, first_other)
    point = pw_out[0]
    point_near = jnp.stack([point] + [along(point, -d, False) for d in range(1, SIDE)])
    point_next, point_before = along(point_near, -1, True), along(point_near, 1, True)

    phases = lax.axis_size("phase")

    def from_behind(value):
        return lax.ppermute(value, "phase", [(i, i - 1) for i in range(1, phases)])

    whole = incoming.reshape(NX, NY, NC, ROWS, width)
    parts = ff_first(after(here, point_near), whole, own_pre, other_pre, weights)
    own_first = lax.dynamic_slice_in_dim(incoming[0], spot * ROWS, ROWS, 0)
    point_next, point_before, _ = lax.optimization_barrier((point_next, point_before, parts[2]))
    half = SIDE // 2
    point_far = along(point_next[:half], -1, True), along(point_before[half:], 1, True)
    mine = jnp.concatenate([point_near, point_next, *point_far, point_before], axis=0)
    point_full = ordered(here, mine, swap_cores(mine))
    residual = scattered(parts, own_first)
    other_pre = other_half(1, after(own_pre, parts[0]))
    taps_behind = from_behind(after(taps_here, parts[0]))
    residual = lax.optimization_barrier((residual, other_pre, taps_behind, point_full))[0]

    residual_behind = from_behind(residual)
    conv_grad = conv_gradient(residual, conv_pre[0, 0], point_full)
    received = with_taps(residual_behind, from_behind(conv_grad), *edges(conv_grad, 1), taps_behind)
    arriving = jnp.where(lax.axis_index("phase") == phases - 1, fresh_grad, received)
    near = jnp.stack([arriving] + [along(arriving, -d, False) for d in range(1, SIDE)])
    conv_grad = after(conv_grad, near)
    first_turn = with_taps(residual, conv_grad, *edges(conv_grad, 0), taps_here)

    back = functools.partial(ff_back, here, 1, own_pre=own_pre, other_pre=other_pre, weights=weights)
    residual = scattered(gathered_back(near, back), arriving)
    conv_grad = conv_gradient(residual, conv_pre[1, 0], point_full)
    second_turn = with_taps(residual, conv_grad, *edges(conv_grad, 0), taps_here)
    return jnp.stack([first_turn, second_turn])[:, None]


def solution(mesh):
    return jax.shard_map(
        per_device,
        mesh=mesh,
        in_specs=(
            P("phase", None, None),
            P("tensor", None),
            P(None, "phase", None, "tensor"),
            P(None, "phase", "tensor", None),
            P("phase", None, "tensor"),
            P("phase", "tensor", None),
            P("phase", "tensor", None),
            P("phase", None, None),
        ),
        out_specs=P(None, "phase", "tensor", None),
        check_vma=False,
    )
```

```python
import functools

import jax
import jax.numpy as jnp
from jax import lax
from jax.experimental import pallas as pl
from jax.experimental.pallas import tpu as pltpu
from jax.sharding import PartitionSpec as P

NX, NY, NC = 4, 4, 2
SIDE, ROWS, EDGE = 4, 64, 16
BF16, F32 = jnp.bfloat16, jnp.float32
CHIPS = [(x, y, c) for x in range(NX) for y in range(NY) for c in range(NC)]


def place(x, y, c):
    return (x % NX * NY + y % NY) * NC + c


def along(value, d, first):
    pairs = []
    for x, y, c in CHIPS:
        dx, dy = (0, d) if (c == 0) == first else (d, 0)
        pairs.append((place(x, y, c), place(x + dx, y + dy, c)))
    return lax.ppermute(value, "tensor", pairs)


def swap_cores(value):
    return lax.ppermute(value, "tensor", [(place(x, y, c), place(x, y, 1 - c)) for x, y, c in CHIPS])


def after(value, *others):
    return lax.optimization_barrier((value, *others))[0]


def gated_back(hidden_grad, activation):
    pre_value = activation.astype(F32)
    sigmoid_a = jax.nn.sigmoid(pre_value)
    return (hidden_grad * sigmoid_a * (1.0 + pre_value * (1.0 - sigmoid_a))).astype(BF16)


def times_transpose(left, right):
    return lax.dot_general(left, right, (((1,), (1,)), ((), ())), preferred_element_type=F32)


def spots(place_ref, d):
    x, y, c = place_ref[0], place_ref[1], place_ref[2]
    found = []
    for k in range(SIDE):
        dx, dy = jnp.where(c == 0, k, d), jnp.where(c == 0, d, k)
        found.append(((x + dx) % NX, (y + dy) % NY))
    return found


def ff_rows(gradient, pre_own, pre_other, out_own, out_other, in_own, in_other):
    gates = [
        gated_back(times_transpose(gradient, second[...]), pre)
        for second, pre in ((out_own, pre_own), (out_other, pre_other))
    ]
    first = jnp.concatenate([in_own[...], in_other[...]], axis=1)
    return times_transpose(jnp.concatenate(gates, axis=1), first).astype(BF16)


def ff_first_body(place_ref, other_pre, out_other, in_other, own_pre, out_own, in_own, grads, *refs):
    results, (held_out, held_in, held_pre, held_grad, sems) = refs[:SIDE], refs[SIDE:]
    c = place_ref[2]
    copies = [
        (grads.at[:, :, c], held_grad),
        (out_own, held_out),
        (own_pre.at[0, :, :, c], held_pre),
        (in_own, held_in),
    ]
    copies = [pltpu.make_async_copy(src, dst, sems.at[i]) for i, (src, dst) in enumerate(copies)]
    for copy in copies:
        copy.start()
    for copy in copies:
        copy.wait()
    for d in (2, 1, 3, 0):
        found = spots(place_ref, d)
        rows = [jnp.concatenate([r[i, j] for i, j in found], axis=0) for r in (held_grad, held_pre, other_pre)]
        results[d][...] = ff_rows(*rows, held_out, out_other, held_in, in_other).reshape(results[d].shape)


def ff_first(here, grads, own_pre, other_pre, weights):
    units, width = weights[0].shape
    rows = SIDE * SIDE * ROWS
    near = [pltpu.with_memory_space_constraint(v, pltpu.VMEM) for v in (other_pre, weights[1], weights[3])]
    far = [pltpu.with_memory_space_constraint(v, pltpu.HBM) for v in (own_pre, weights[0], weights[2], grads)]
    return pl.pallas_call(
        ff_first_body,
        in_specs=[pl.BlockSpec(memory_space=pltpu.SMEM)]
        + [pl.BlockSpec(memory_space=pltpu.VMEM)] * 3
        + [pl.BlockSpec(memory_space=pltpu.HBM)] * 4,
        out_specs=[pl.BlockSpec(memory_space=pltpu.VMEM)] * SIDE,
        out_shape=[jax.ShapeDtypeStruct((SIDE, ROWS, width), BF16)] * SIDE,
        scratch_shapes=[
            pltpu.VMEM(weights[0].shape, BF16),
            pltpu.VMEM(weights[2].shape, BF16),
            pltpu.VMEM((NX, NY, ROWS, units), BF16),
            pltpu.VMEM((NX, NY, ROWS, width), BF16),
            pltpu.SemaphoreType.DMA((4,)),
        ],
        compiler_params=pltpu.CompilerParams(vmem_limit_bytes=32 * 1024 * 1024),
        cost_estimate=pl.CostEstimate(
            flops=8 * rows * width * units,
            bytes_accessed=8 * units * width + 4 * rows * width,
            transcendentals=2 * rows * units,
        ),
        name="ff_first",
    )(here, *near, *far)


def pack_body(*refs):
    into, at = refs[-1], 0
    for ref in refs[:-1]:
        into[at : at + ref.shape[0]] = ref[...]
        at += ref.shape[0]


def packed(*pieces):
    shape = (sum(p.shape[0] for p in pieces), *pieces[0].shape[1:])
    pieces = [pltpu.with_memory_space_constraint(p, pltpu.VMEM) for p in pieces]
    inside = pl.BlockSpec(memory_space=pltpu.VMEM)
    return pl.pallas_call(
        pack_body,
        in_specs=[inside] * len(pieces),
        out_specs=inside,
        out_shape=jax.ShapeDtypeStruct(shape, BF16),
        compiler_params=pltpu.CompilerParams(vmem_limit_bytes=16 * 1024 * 1024),
        cost_estimate=pl.CostEstimate(flops=0, bytes_accessed=4 * shape[0] * shape[1] * shape[2], transcendentals=0),
        name="pack",
    )(*pieces)


def order_body(place_ref, mine, other, full):
    x, y, c = place_ref[0], place_ref[1], place_ref[2]
    height = mine.shape[1]
    for source, core in ((mine, c), (other, 1 - c)):
        for a in range(SIDE):
            for b in range(SIDE):
                dx, dy = jnp.where(core == 0, b, a), jnp.where(core == 0, a, b)
                row = (((x + dx) % NX * NY + (y + dy) % NY) * NC + core) * height
                full[pl.ds(pl.multiple_of(row, height), height)] = source[a * SIDE + b]


def ordered(here, mine, other):
    count, height, width = mine.shape
    mine, other = [pltpu.with_memory_space_constraint(v, pltpu.VMEM) for v in (mine, other)]
    inside = pl.BlockSpec(memory_space=pltpu.VMEM)
    return pl.pallas_call(
        order_body,
        in_specs=[pl.BlockSpec(memory_space=pltpu.SMEM), inside, inside],
        out_specs=inside,
        out_shape=jax.ShapeDtypeStruct((NC * count * height, width), BF16),
        compiler_params=pltpu.CompilerParams(vmem_limit_bytes=16 * 1024 * 1024),
        cost_estimate=pl.CostEstimate(flops=0, bytes_accessed=4 * NC * count * height * width, transcendentals=0),
        name="order",
    )(here, mine, other)


def ff_body(turn, dists, place_ref, own_pre, other_pre, *refs):
    weights, refs = refs[:4], refs[4:]
    results, g_refs = refs[-len(dists) :], refs[: -len(dists)]
    found = [spot for d in dists for spot in spots(place_ref, d)]
    c = place_ref[2]
    gradient = jnp.concatenate([r[...].reshape(-1, r.shape[-1]) for r in g_refs], axis=0)
    pre_own = jnp.concatenate([own_pre[turn, i, j, c] for i, j in found], axis=0)
    pre_other = jnp.concatenate([other_pre[i, j] for i, j in found], axis=0)
    partial = ff_rows(gradient, pre_own, pre_other, *weights)
    size = SIDE * ROWS
    for i, result in enumerate(results):
        result[...] = partial[i * size : (i + 1) * size].reshape(result.shape)


def ff_back(here, turn, dists, grads, own_pre, other_pre, weights):
    units, width = weights[0].shape
    rows = SIDE * ROWS * len(dists)
    operands = [own_pre, other_pre, *weights, *grads]
    operands = [pltpu.with_memory_space_constraint(v, pltpu.VMEM) for v in operands]
    inside = pl.BlockSpec(memory_space=pltpu.VMEM)
    return pl.pallas_call(
        functools.partial(ff_body, turn, dists),
        in_specs=[pl.BlockSpec(memory_space=pltpu.SMEM)] + [inside] * len(operands),
        out_specs=[inside] * len(dists),
        out_shape=[jax.ShapeDtypeStruct((SIDE, ROWS, width), BF16)] * len(dists),
        compiler_params=pltpu.CompilerParams(vmem_limit_bytes=24 * 1024 * 1024),
        cost_estimate=pl.CostEstimate(
            flops=8 * rows * width * units,
            bytes_accessed=8 * units * width + 4 * rows * width,
            transcendentals=2 * rows * units,
        ),
        name="ff_back",
    )(here, *operands)


def gathered_back(near, back):
    following, previous = along(near, -1, True), along(near, 1, True)
    half = near.shape[0] // 2
    (p0,) = back((0,), [near])
    following, previous, p0 = lax.optimization_barrier((following, previous, p0))
    opposite = along(following[:half], -1, True), along(previous[half:], 1, True)
    p1, p3 = back((1, 3), [following, previous])
    *opposite, p1 = lax.optimization_barrier((*opposite, p1))
    (p2,) = back((2,), opposite)
    return p0, p1, p2, p3


def scattered(got, own, *awaited):
    total = sum(v.astype(F32) for v in got)
    send = total.astype(BF16)
    got = [along(send[d], d, False) for d in (2, 1, 3)]
    if awaited:
        got = lax.optimization_barrier((*got, *awaited))[: len(got)]
    return (own.astype(F32) + total[0] + sum(v.astype(F32) for v in got)).astype(BF16)


def conv_gradient(residual, conv_in, point_full):
    swish_grad = times_transpose(residual, point_full).astype(BF16)
    return gated_back(swish_grad.astype(F32), conv_in)


def edges(block):
    count = lax.axis_size("tensor")
    forward = [(i, i + 1) for i in range(count - 1)]
    backward = [(target, source) for source, target in forward]
    return lax.ppermute(block[-EDGE:], "tensor", forward), lax.ppermute(block[:EDGE], "tensor", backward)


def rows_of(taps):
    return [taps[i] for i in range(taps.shape[0])]


def with_taps(residual, conv_grad, low, high, taps):
    row_count, last = residual.shape[0], len(taps) - 1
    padded = jnp.concatenate([low, conv_grad, high], axis=0)
    running = jnp.zeros(residual.shape, F32)
    for tap_index in range(last + 1):
        offset_row = EDGE + last // 2 - tap_index
        running = running + taps[tap_index] * padded[offset_row : offset_row + row_count].astype(F32)
    return (residual.astype(F32) + running).astype(BF16)


def per_device(incoming, fresh_grad, pre_act, conv_pre, w_in, w_out, pw_out, kernel):
    first_proj, second_proj, taps_here = w_in[0], w_out[0], kernel[0]
    spot = lax.axis_index("tensor")
    x, y, c = spot // (NY * NC), spot // NC % NY, spot % NC
    here = jnp.stack([x, y, c]).astype(jnp.int32)
    units, width = second_proj.shape

    own_pre = pre_act.reshape(2, NX, NY, NC, ROWS, units)

    def other_rows(source, turn):
        rows = lax.dynamic_slice(source, (turn, 0, 0, 1 - c, 0, 0), (1, NX, NY, 1, ROWS, units))
        return rows.reshape(NX, NY, ROWS, units)

    point = pw_out[0]
    point_got = [along(point, -d, False) for d in (1, 2, 3)]
    other_pre = swap_cores(other_rows(own_pre, 0))
    second_other = swap_cores(second_proj)
    first_other = swap_cores(first_proj)
    weights = (second_proj, second_other, first_proj, first_other)
    whole = incoming.reshape(NX, NY, NC, ROWS, width)
    parts = ff_first(here, whole, own_pre, other_pre, weights)
    got = [along(parts[d], d, True) for d in (2, 1, 3)]
    own_first = lax.dynamic_slice_in_dim(incoming[0], spot * ROWS, ROWS, 0)
    *point_got, _ = lax.optimization_barrier((*point_got, parts[2]))
    point_near = packed(*[v[None] for v in (point, *point_got)])
    point_next, point_before = along(point_near, -1, True), along(point_near, 1, True)
    half = SIDE // 2
    point_far = along(point_next[:half], -1, True), along(point_before[half:], 1, True)
    *point_far, _, _, _ = lax.optimization_barrier((*point_far, *got))
    mine = packed(point_near, point_next, *point_far, point_before)
    point_full = ordered(here, mine, swap_cores(mine))
    residual = scattered([parts[0], *got], own_first, point_full)
    other_pre = swap_cores(other_rows(after(own_pre, parts[0]), 1))
    residual, _, *taps = lax.optimization_barrier((residual, other_pre, *rows_of(taps_here)))

    phases = lax.axis_size("phase")
    conv_grad = conv_gradient(residual, conv_pre[0, 0], point_full)
    first_turn = with_taps(residual, conv_grad, *edges(conv_grad), taps)
    received = lax.ppermute(first_turn, "phase", [(i, i - 1) for i in range(1, phases)])
    arriving = jnp.where(lax.axis_index("phase") == phases - 1, fresh_grad, received)
    near = packed(*[v[None] for v in (arriving, *[along(arriving, -d, False) for d in range(1, SIDE)])])

    back = functools.partial(ff_back, here, 1, own_pre=own_pre, other_pre=other_pre, weights=weights)
    p0, p1, p2, p3 = gathered_back(near, back)
    residual = scattered([p0, along(p1, 1, True), along(p3, 3, True), along(p2, 2, True)], arriving)
    both = jnp.pad(first_turn[None, None], ((0, 1), (0, 0), (0, 0), (0, 0)))
    residual, both = lax.optimization_barrier((residual, both))
    conv_grad = conv_gradient(residual, conv_pre[1, 0], point_full)
    second_turn = with_taps(residual, conv_grad, *edges(conv_grad), taps)
    return lax.dynamic_update_slice(both, second_turn[None, None], (1, 0, 0, 0))


def solution(mesh):
    return jax.shard_map(
        per_device,
        mesh=mesh,
        in_specs=(
            P("phase", None, None),
            P("tensor", None),
            P(None, "phase", None, "tensor"),
            P(None, "phase", "tensor", None),
            P("phase", None, "tensor"),
            P("phase", "tensor", None),
            P("phase", "tensor", None),
            P("phase", None, None),
        ),
        out_specs=P(None, "phase", "tensor", None),
        check_vma=False,
    )
```

```python
import functools

import jax
import jax.numpy as jnp
from jax import lax
from jax.experimental import pallas as pl
from jax.experimental.pallas import tpu as pltpu
from jax.sharding import PartitionSpec as P

NX, NY, NC = 4, 4, 2
SIDE, ROWS, EDGE = 4, 64, 16
BF16, F32 = jnp.bfloat16, jnp.float32
CHIPS = [(x, y, c) for x in range(NX) for y in range(NY) for c in range(NC)]


def place(x, y, c):
    return (x % NX * NY + y % NY) * NC + c


def along(value, d, first):
    pairs = []
    for x, y, c in CHIPS:
        dx, dy = (0, d) if (c == 0) == first else (d, 0)
        pairs.append((place(x, y, c), place(x + dx, y + dy, c)))
    return lax.ppermute(value, "tensor", pairs)


def swap_cores(value):
    return lax.ppermute(value, "tensor", [(place(x, y, c), place(x, y, 1 - c)) for x, y, c in CHIPS])


def after(value, *others):
    return lax.optimization_barrier((value, *others))[0]


def gated_back(hidden_grad, activation):
    pre_value = activation.astype(F32)
    sigmoid_a = jax.nn.sigmoid(pre_value)
    return (hidden_grad * sigmoid_a * (1.0 + pre_value * (1.0 - sigmoid_a))).astype(BF16)


def times_transpose(left, right):
    return lax.dot_general(left, right, (((1,), (1,)), ((), ())), preferred_element_type=F32)


def spots(place_ref, d):
    x, y, c = place_ref[0], place_ref[1], place_ref[2]
    found = []
    for k in range(SIDE):
        dx, dy = jnp.where(c == 0, k, d), jnp.where(c == 0, d, k)
        found.append(((x + dx) % NX, (y + dy) % NY))
    return found


def ff_rows(gradient, pre_own, pre_other, out_own, out_other, in_own, in_other):
    gates = [
        gated_back(times_transpose(gradient, second[...]), pre)
        for second, pre in ((out_own, pre_own), (out_other, pre_other))
    ]
    first = jnp.concatenate([in_own[...], in_other[...]], axis=1)
    return times_transpose(jnp.concatenate(gates, axis=1), first).astype(BF16)


def ff_first_body(place_ref, other_pre, out_other, in_other, own_pre, out_own, in_own, grads, *refs):
    results, (held_out, held_in, held_pre, held_grad, sems) = refs[:SIDE], refs[SIDE:]
    c = place_ref[2]
    copies = [
        (grads.at[:, :, c], held_grad),
        (out_own, held_out),
        (own_pre.at[0, :, :, c], held_pre),
        (in_own, held_in),
    ]
    copies = [pltpu.make_async_copy(src, dst, sems.at[i]) for i, (src, dst) in enumerate(copies)]
    for copy in copies:
        copy.start()
    for copy in copies:
        copy.wait()
    for d in (2, 1, 3, 0):
        found = spots(place_ref, d)
        rows = [jnp.concatenate([r[i, j] for i, j in found], axis=0) for r in (held_grad, held_pre, other_pre)]
        results[d][...] = ff_rows(*rows, held_out, out_other, held_in, in_other).reshape(results[d].shape)


def ff_first(here, grads, own_pre, other_pre, weights):
    units, width = weights[0].shape
    rows = SIDE * SIDE * ROWS
    near = [pltpu.with_memory_space_constraint(v, pltpu.VMEM) for v in (other_pre, weights[1], weights[3])]
    far = [pltpu.with_memory_space_constraint(v, pltpu.HBM) for v in (own_pre, weights[0], weights[2], grads)]
    return pl.pallas_call(
        ff_first_body,
        in_specs=[pl.BlockSpec(memory_space=pltpu.SMEM)]
        + [pl.BlockSpec(memory_space=pltpu.VMEM)] * 3
        + [pl.BlockSpec(memory_space=pltpu.HBM)] * 4,
        out_specs=[pl.BlockSpec(memory_space=pltpu.VMEM)] * SIDE,
        out_shape=[jax.ShapeDtypeStruct((SIDE, ROWS, width), BF16)] * SIDE,
        scratch_shapes=[
            pltpu.VMEM(weights[0].shape, BF16),
            pltpu.VMEM(weights[2].shape, BF16),
            pltpu.VMEM((NX, NY, ROWS, units), BF16),
            pltpu.VMEM((NX, NY, ROWS, width), BF16),
            pltpu.SemaphoreType.DMA((4,)),
        ],
        compiler_params=pltpu.CompilerParams(vmem_limit_bytes=32 * 1024 * 1024),
        cost_estimate=pl.CostEstimate(
            flops=8 * rows * width * units,
            bytes_accessed=8 * units * width + 4 * rows * width,
            transcendentals=2 * rows * units,
        ),
        name="ff_first",
    )(here, *near, *far)


def pack_body(*refs):
    into, at = refs[-1], 0
    for ref in refs[:-1]:
        into[at : at + ref.shape[0]] = ref[...]
        at += ref.shape[0]


def packed(*pieces):
    shape = (sum(p.shape[0] for p in pieces), *pieces[0].shape[1:])
    pieces = [pltpu.with_memory_space_constraint(p, pltpu.VMEM) for p in pieces]
    inside = pl.BlockSpec(memory_space=pltpu.VMEM)
    return pl.pallas_call(
        pack_body,
        in_specs=[inside] * len(pieces),
        out_specs=inside,
        out_shape=jax.ShapeDtypeStruct(shape, BF16),
        compiler_params=pltpu.CompilerParams(vmem_limit_bytes=16 * 1024 * 1024),
        cost_estimate=pl.CostEstimate(flops=0, bytes_accessed=4 * shape[0] * shape[1] * shape[2], transcendentals=0),
        name="pack",
    )(*pieces)


def order_body(place_ref, mine, other, full):
    x, y, c = place_ref[0], place_ref[1], place_ref[2]
    height = mine.shape[1]
    for source, core in ((mine, c), (other, 1 - c)):
        for a in range(SIDE):
            for b in range(SIDE):
                dx, dy = jnp.where(core == 0, b, a), jnp.where(core == 0, a, b)
                row = (((x + dx) % NX * NY + (y + dy) % NY) * NC + core) * height
                full[pl.ds(pl.multiple_of(row, height), height)] = source[a * SIDE + b]


def ordered(here, mine, other):
    count, height, width = mine.shape
    mine, other = [pltpu.with_memory_space_constraint(v, pltpu.VMEM) for v in (mine, other)]
    inside = pl.BlockSpec(memory_space=pltpu.VMEM)
    return pl.pallas_call(
        order_body,
        in_specs=[pl.BlockSpec(memory_space=pltpu.SMEM), inside, inside],
        out_specs=inside,
        out_shape=jax.ShapeDtypeStruct((NC * count * height, width), BF16),
        compiler_params=pltpu.CompilerParams(vmem_limit_bytes=16 * 1024 * 1024),
        cost_estimate=pl.CostEstimate(flops=0, bytes_accessed=4 * NC * count * height * width, transcendentals=0),
        name="order",
    )(here, mine, other)


def ff_body(turn, dists, place_ref, own_pre, other_pre, *refs):
    weights, refs = refs[:4], refs[4:]
    results, g_refs = refs[-len(dists) :], refs[: -len(dists)]
    found = [spot for d in dists for spot in spots(place_ref, d)]
    c = place_ref[2]
    gradient = jnp.concatenate([r[...].reshape(-1, r.shape[-1]) for r in g_refs], axis=0)
    pre_own = jnp.concatenate([own_pre[turn, i, j, c] for i, j in found], axis=0)
    pre_other = jnp.concatenate([other_pre[i, j] for i, j in found], axis=0)
    partial = ff_rows(gradient, pre_own, pre_other, *weights)
    size = SIDE * ROWS
    for i, result in enumerate(results):
        result[...] = partial[i * size : (i + 1) * size].reshape(result.shape)


def ff_back(here, turn, dists, grads, own_pre, other_pre, weights):
    units, width = weights[0].shape
    rows = SIDE * ROWS * len(dists)
    operands = [own_pre, other_pre, *weights, *grads]
    operands = [pltpu.with_memory_space_constraint(v, pltpu.VMEM) for v in operands]
    inside = pl.BlockSpec(memory_space=pltpu.VMEM)
    return pl.pallas_call(
        functools.partial(ff_body, turn, dists),
        in_specs=[pl.BlockSpec(memory_space=pltpu.SMEM)] + [inside] * len(operands),
        out_specs=[inside] * len(dists),
        out_shape=[jax.ShapeDtypeStruct((SIDE, ROWS, width), BF16)] * len(dists),
        compiler_params=pltpu.CompilerParams(vmem_limit_bytes=24 * 1024 * 1024),
        cost_estimate=pl.CostEstimate(
            flops=8 * rows * width * units,
            bytes_accessed=8 * units * width + 4 * rows * width,
            transcendentals=2 * rows * units,
        ),
        name="ff_back",
    )(here, *operands)


def gathered_back(near, back):
    following, previous = along(near, -1, True), along(near, 1, True)
    half = near.shape[0] // 2
    (p0,) = back((0,), [near])
    following, previous, p0 = lax.optimization_barrier((following, previous, p0))
    opposite = along(following[:half], -1, True), along(previous[half:], 1, True)
    p1, p3 = back((1, 3), [following, previous])
    *opposite, p1 = lax.optimization_barrier((*opposite, p1))
    (p2,) = back((2,), opposite)
    return p0, p1, p2, p3


def scattered(got, own, *awaited):
    total = sum(v.astype(F32) for v in got)
    send = total.astype(BF16)
    got = [along(send[d], d, False) for d in (2, 1, 3)]
    if awaited:
        got = lax.optimization_barrier((*got, *awaited))[: len(got)]
    return (own.astype(F32) + total[0] + sum(v.astype(F32) for v in got)).astype(BF16)


def conv_gradient(residual, conv_in, point_full):
    swish_grad = times_transpose(residual, point_full).astype(BF16)
    return gated_back(swish_grad.astype(F32), conv_in)


def edges(block):
    count = lax.axis_size("tensor")
    forward = [(i, i + 1) for i in range(count - 1)]
    backward = [(target, source) for source, target in forward]
    return lax.ppermute(block[-EDGE:], "tensor", forward), lax.ppermute(block[:EDGE], "tensor", backward)


def rows_of(taps):
    return [taps[i] for i in range(taps.shape[0])]


def with_taps(residual, conv_grad, low, high, taps):
    row_count, last = residual.shape[0], len(taps) - 1
    padded = jnp.concatenate([low, conv_grad, high], axis=0)
    running = jnp.zeros(residual.shape, F32)
    for tap_index in range(last + 1):
        offset_row = EDGE + last // 2 - tap_index
        running = running + taps[tap_index] * padded[offset_row : offset_row + row_count].astype(F32)
    return (residual.astype(F32) + running).astype(BF16)


def per_device(incoming, fresh_grad, pre_act, conv_pre, w_in, w_out, pw_out, kernel):
    first_proj, second_proj, taps_here = w_in[0], w_out[0], kernel[0]
    spot = lax.axis_index("tensor")
    x, y, c = spot // (NY * NC), spot // NC % NY, spot % NC
    here = jnp.stack([x, y, c]).astype(jnp.int32)
    units, width = second_proj.shape

    own_pre = pre_act.reshape(2, NX, NY, NC, ROWS, units)

    def other_rows(source, turn):
        rows = lax.dynamic_slice(source, (turn, 0, 0, 1 - c, 0, 0), (1, NX, NY, 1, ROWS, units))
        return rows.reshape(NX, NY, ROWS, units)

    point = pw_out[0]
    point_got = [along(point, -d, False) for d in (1, 2, 3)]
    other_pre = swap_cores(other_rows(own_pre, 0))
    second_other = swap_cores(second_proj)
    first_other = swap_cores(first_proj)
    weights = (second_proj, second_other, first_proj, first_other)
    whole = incoming.reshape(NX, NY, NC, ROWS, width)
    parts = ff_first(here, whole, own_pre, other_pre, weights)
    got = [along(parts[d], d, True) for d in (2, 1, 3)]
    own_first = lax.dynamic_slice_in_dim(incoming[0], spot * ROWS, ROWS, 0)
    *point_got, _ = lax.optimization_barrier((*point_got, parts[2]))
    point_near = packed(*[v[None] for v in (point, *point_got)])
    point_next, point_before = along(point_near, -1, True), along(point_near, 1, True)
    half = SIDE // 2
    point_far = along(point_next[:half], -1, True), along(point_before[half:], 1, True)
    *point_far, _, _, _ = lax.optimization_barrier((*point_far, *got))
    mine = packed(point_near, point_next, *point_far, point_before)
    point_full = ordered(here, mine, swap_cores(mine))
    residual = scattered([parts[0], *got], own_first, point_full)
    other_pre = swap_cores(other_rows(after(own_pre, parts[0]), 1))
    residual, _, *taps = lax.optimization_barrier((residual, other_pre, *rows_of(taps_here)))

    phases = lax.axis_size("phase")
    conv_grad = conv_gradient(residual, conv_pre[0, 0], point_full)
    first_turn = with_taps(residual, conv_grad, *edges(conv_grad), taps)
    received = lax.ppermute(first_turn, "phase", [(i, i - 1) for i in range(1, phases)])
    arriving = jnp.where(lax.axis_index("phase") == phases - 1, fresh_grad, received)
    near = packed(*[v[None] for v in (arriving, *[along(arriving, -d, False) for d in range(1, SIDE)])])

    back = functools.partial(ff_back, here, 1, own_pre=own_pre, other_pre=other_pre, weights=weights)
    p0, p1, p2, p3 = gathered_back(near, back)
    early = lax.optimization_barrier(sum(v.astype(F32) for v in (p0, along(p1, 1, True), along(p3, 3, True))))
    residual = scattered([early, along(p2, 2, True)], arriving)
    both = jnp.pad(first_turn[None, None], ((0, 1), (0, 0), (0, 0), (0, 0)))
    residual, both = lax.optimization_barrier((residual, both))
    conv_grad = conv_gradient(residual, conv_pre[1, 0], point_full)
    second_turn = with_taps(residual, conv_grad, *edges(conv_grad), taps)
    return lax.dynamic_update_slice(both, second_turn[None, None], (1, 0, 0, 0))


def solution(mesh):
    return jax.shard_map(
        per_device,
        mesh=mesh,
        in_specs=(
            P("phase", None, None),
            P("tensor", None),
            P(None, "phase", None, "tensor"),
            P(None, "phase", "tensor", None),
            P("phase", None, "tensor"),
            P("phase", "tensor", None),
            P("phase", "tensor", None),
            P("phase", None, None),
        ),
        out_specs=P(None, "phase", "tensor", None),
        check_vma=False,
    )
```

```python
import functools

import jax
import jax.numpy as jnp
from jax import lax
from jax.experimental import pallas as pl
from jax.experimental.pallas import tpu as pltpu
from jax.sharding import PartitionSpec as P

NX, NY, NC = 4, 4, 2
SIDE, ROWS, EDGE = 4, 64, 16
BF16, F32 = jnp.bfloat16, jnp.float32
CHIPS = [(x, y, c) for x in range(NX) for y in range(NY) for c in range(NC)]


def place(x, y, c):
    return (x % NX * NY + y % NY) * NC + c


def along(value, d, first):
    pairs = []
    for x, y, c in CHIPS:
        dx, dy = (0, d) if (c == 0) == first else (d, 0)
        pairs.append((place(x, y, c), place(x + dx, y + dy, c)))
    return lax.ppermute(value, "tensor", pairs)


def swap_cores(value):
    return lax.ppermute(value, "tensor", [(place(x, y, c), place(x, y, 1 - c)) for x, y, c in CHIPS])


def after(value, *others):
    return lax.optimization_barrier((value, *others))[0]


def gated_back(hidden_grad, activation):
    pre_value = activation.astype(F32)
    sigmoid_a = jax.nn.sigmoid(pre_value)
    return (hidden_grad * sigmoid_a * (1.0 + pre_value * (1.0 - sigmoid_a))).astype(BF16)


def times_transpose(left, right):
    return lax.dot_general(left, right, (((1,), (1,)), ((), ())), preferred_element_type=F32)


def spots(place_ref, d):
    x, y, c = place_ref[0], place_ref[1], place_ref[2]
    found = []
    for k in range(SIDE):
        dx, dy = jnp.where(c == 0, k, d), jnp.where(c == 0, d, k)
        found.append(((x + dx) % NX, (y + dy) % NY))
    return found


def ff_rows(gradient, pre_own, pre_other, out_own, out_other, in_own, in_other):
    gates = [
        gated_back(times_transpose(gradient, second[...]), pre)
        for second, pre in ((out_own, pre_own), (out_other, pre_other))
    ]
    first = jnp.concatenate([in_own[...], in_other[...]], axis=1)
    return times_transpose(jnp.concatenate(gates, axis=1), first).astype(BF16)


def ff_first_body(place_ref, other_pre, out_other, in_other, own_pre, out_own, in_own, grads, *refs):
    results, (held_out, held_in, held_pre, held_grad, sems) = refs[:SIDE], refs[SIDE:]
    c = place_ref[2]
    copies = [
        (grads.at[:, :, c], held_grad),
        (out_own, held_out),
        (own_pre.at[0, :, :, c], held_pre),
        (in_own, held_in),
    ]
    copies = [pltpu.make_async_copy(src, dst, sems.at[i]) for i, (src, dst) in enumerate(copies)]
    for copy in copies:
        copy.start()
    for copy in copies:
        copy.wait()
    for d in (2, 1, 3, 0):
        found = spots(place_ref, d)
        rows = [jnp.concatenate([r[i, j] for i, j in found], axis=0) for r in (held_grad, held_pre, other_pre)]
        results[d][...] = ff_rows(*rows, held_out, out_other, held_in, in_other).reshape(results[d].shape)


def ff_first(here, grads, own_pre, other_pre, weights):
    units, width = weights[0].shape
    rows = SIDE * SIDE * ROWS
    near = [pltpu.with_memory_space_constraint(v, pltpu.VMEM) for v in (other_pre, weights[1], weights[3])]
    far = [pltpu.with_memory_space_constraint(v, pltpu.HBM) for v in (own_pre, weights[0], weights[2], grads)]
    return pl.pallas_call(
        ff_first_body,
        in_specs=[pl.BlockSpec(memory_space=pltpu.SMEM)]
        + [pl.BlockSpec(memory_space=pltpu.VMEM)] * 3
        + [pl.BlockSpec(memory_space=pltpu.HBM)] * 4,
        out_specs=[pl.BlockSpec(memory_space=pltpu.VMEM)] * SIDE,
        out_shape=[jax.ShapeDtypeStruct((SIDE, ROWS, width), BF16)] * SIDE,
        scratch_shapes=[
            pltpu.VMEM(weights[0].shape, BF16),
            pltpu.VMEM(weights[2].shape, BF16),
            pltpu.VMEM((NX, NY, ROWS, units), BF16),
            pltpu.VMEM((NX, NY, ROWS, width), BF16),
            pltpu.SemaphoreType.DMA((4,)),
        ],
        compiler_params=pltpu.CompilerParams(vmem_limit_bytes=32 * 1024 * 1024),
        cost_estimate=pl.CostEstimate(
            flops=8 * rows * width * units,
            bytes_accessed=8 * units * width + 4 * rows * width,
            transcendentals=2 * rows * units,
        ),
        name="ff_first",
    )(here, *near, *far)


def pack_body(*refs):
    into, at = refs[-1], 0
    for ref in refs[:-1]:
        into[at : at + ref.shape[0]] = ref[...]
        at += ref.shape[0]


def packed(*pieces):
    shape = (sum(p.shape[0] for p in pieces), *pieces[0].shape[1:])
    pieces = [pltpu.with_memory_space_constraint(p, pltpu.VMEM) for p in pieces]
    inside = pl.BlockSpec(memory_space=pltpu.VMEM)
    return pl.pallas_call(
        pack_body,
        in_specs=[inside] * len(pieces),
        out_specs=inside,
        out_shape=jax.ShapeDtypeStruct(shape, BF16),
        compiler_params=pltpu.CompilerParams(vmem_limit_bytes=16 * 1024 * 1024),
        cost_estimate=pl.CostEstimate(flops=0, bytes_accessed=4 * shape[0] * shape[1] * shape[2], transcendentals=0),
        name="pack",
    )(*pieces)


def order_body(place_ref, mine, other, full):
    x, y, c = place_ref[0], place_ref[1], place_ref[2]
    height = mine.shape[1]
    for source, core in ((mine, c), (other, 1 - c)):
        for a in range(SIDE):
            for b in range(SIDE):
                dx, dy = jnp.where(core == 0, b, a), jnp.where(core == 0, a, b)
                row = (((x + dx) % NX * NY + (y + dy) % NY) * NC + core) * height
                full[pl.ds(pl.multiple_of(row, height), height)] = source[a * SIDE + b]


def ordered(here, mine, other):
    count, height, width = mine.shape
    mine, other = [pltpu.with_memory_space_constraint(v, pltpu.VMEM) for v in (mine, other)]
    inside = pl.BlockSpec(memory_space=pltpu.VMEM)
    return pl.pallas_call(
        order_body,
        in_specs=[pl.BlockSpec(memory_space=pltpu.SMEM), inside, inside],
        out_specs=inside,
        out_shape=jax.ShapeDtypeStruct((NC * count * height, width), BF16),
        compiler_params=pltpu.CompilerParams(vmem_limit_bytes=16 * 1024 * 1024),
        cost_estimate=pl.CostEstimate(flops=0, bytes_accessed=4 * NC * count * height * width, transcendentals=0),
        name="order",
    )(here, mine, other)


def ff_body(turn, dists, place_ref, own_pre, other_pre, *refs):
    weights, refs = refs[:4], refs[4:]
    results, g_refs = refs[-len(dists) :], refs[: -len(dists)]
    found = [spot for d in dists for spot in spots(place_ref, d)]
    c = place_ref[2]
    gradient = jnp.concatenate([r[...].reshape(-1, r.shape[-1]) for r in g_refs], axis=0)
    pre_own = jnp.concatenate([own_pre[turn, i, j, c] for i, j in found], axis=0)
    pre_other = jnp.concatenate([other_pre[i, j] for i, j in found], axis=0)
    partial = ff_rows(gradient, pre_own, pre_other, *weights)
    size = SIDE * ROWS
    for i, result in enumerate(results):
        result[...] = partial[i * size : (i + 1) * size].reshape(result.shape)


def ff_back(here, turn, dists, grads, own_pre, other_pre, weights):
    units, width = weights[0].shape
    rows = SIDE * ROWS * len(dists)
    operands = [own_pre, other_pre, *weights, *grads]
    operands = [pltpu.with_memory_space_constraint(v, pltpu.VMEM) for v in operands]
    inside = pl.BlockSpec(memory_space=pltpu.VMEM)
    return pl.pallas_call(
        functools.partial(ff_body, turn, dists),
        in_specs=[pl.BlockSpec(memory_space=pltpu.SMEM)] + [inside] * len(operands),
        out_specs=[inside] * len(dists),
        out_shape=[jax.ShapeDtypeStruct((SIDE, ROWS, width), BF16)] * len(dists),
        compiler_params=pltpu.CompilerParams(vmem_limit_bytes=24 * 1024 * 1024),
        cost_estimate=pl.CostEstimate(
            flops=8 * rows * width * units,
            bytes_accessed=8 * units * width + 4 * rows * width,
            transcendentals=2 * rows * units,
        ),
        name="ff_back",
    )(here, *operands)


def gathered_back(near, back):
    following, previous = along(near, -1, True), along(near, 1, True)
    half = near.shape[0] // 2
    (p0,) = back((0,), [near])
    following, previous, p0 = lax.optimization_barrier((following, previous, p0))
    opposite = along(following[:half], -1, True), along(previous[half:], 1, True)
    p1, p3 = back((1, 3), [following, previous])
    *opposite, p1 = lax.optimization_barrier((*opposite, p1))
    (p2,) = back((2,), opposite)
    return p0, p1, p2, p3


def scattered(got, own, *awaited):
    total = sum(v.astype(F32) for v in got)
    send = total.astype(BF16)
    got = [along(send[d], d, False) for d in (2, 1, 3)]
    if awaited:
        got = lax.optimization_barrier((*got, *awaited))[: len(got)]
    return (own.astype(F32) + total[0] + sum(v.astype(F32) for v in got)).astype(BF16)


def conv_gradient(residual, conv_in, point_full):
    swish_grad = times_transpose(residual, point_full).astype(BF16)
    return gated_back(swish_grad.astype(F32), conv_in)


def edges(block):
    count = lax.axis_size("tensor")
    forward = [(i, i + 1) for i in range(count - 1)]
    backward = [(target, source) for source, target in forward]
    return lax.ppermute(block[-EDGE:], "tensor", forward), lax.ppermute(block[:EDGE], "tensor", backward)


def rows_of(taps):
    return [taps[i] for i in range(taps.shape[0])]


def with_taps(residual, conv_grad, low, high, taps):
    row_count, last = residual.shape[0], len(taps) - 1
    padded = jnp.concatenate([low, conv_grad, high], axis=0)
    running = jnp.zeros(residual.shape, F32)
    for tap_index in range(last + 1):
        offset_row = EDGE + last // 2 - tap_index
        running = running + taps[tap_index] * padded[offset_row : offset_row + row_count].astype(F32)
    return (residual.astype(F32) + running).astype(BF16)


def per_device(incoming, fresh_grad, pre_act, conv_pre, w_in, w_out, pw_out, kernel):
    first_proj, second_proj, taps_here = w_in[0], w_out[0], kernel[0]
    spot = lax.axis_index("tensor")
    x, y, c = spot // (NY * NC), spot // NC % NY, spot % NC
    here = jnp.stack([x, y, c]).astype(jnp.int32)
    units, width = second_proj.shape

    own_pre = pre_act.reshape(2, NX, NY, NC, ROWS, units)

    def other_rows(source, turn):
        rows = lax.dynamic_slice(source, (turn, 0, 0, 1 - c, 0, 0), (1, NX, NY, 1, ROWS, units))
        return rows.reshape(NX, NY, ROWS, units)

    point = pw_out[0]
    point_got = [along(point, -d, False) for d in (1, 2, 3)]
    other_pre = swap_cores(other_rows(own_pre, 0))
    second_other = swap_cores(second_proj)
    first_other = swap_cores(first_proj)
    weights = (second_proj, second_other, first_proj, first_other)
    whole = incoming.reshape(NX, NY, NC, ROWS, width)
    parts = ff_first(here, whole, own_pre, other_pre, weights)
    got = [along(parts[d], d, True) for d in (2, 1, 3)]
    own_first = lax.dynamic_slice_in_dim(incoming[0], spot * ROWS, ROWS, 0)
    *point_got, _ = lax.optimization_barrier((*point_got, parts[2]))
    point_near = packed(*[v[None] for v in (point, *point_got)])
    point_next, point_before = along(point_near, -1, True), along(point_near, 1, True)
    half = SIDE // 2
    point_far = along(point_next[:half], -1, True), along(point_before[half:], 1, True)
    *point_far, _, _, _ = lax.optimization_barrier((*point_far, *got))
    mine = packed(point_near, point_next, *point_far, point_before)
    point_full = ordered(here, mine, swap_cores(mine))
    early = lax.optimization_barrier(sum(v.astype(F32) for v in (parts[0], *got[1:])))
    residual = scattered([early, got[0]], own_first, point_full)
    other_pre = swap_cores(other_rows(after(own_pre, parts[0]), 1))
    residual, _, *taps = lax.optimization_barrier((residual, other_pre, *rows_of(taps_here)))

    phases = lax.axis_size("phase")
    conv_grad = conv_gradient(residual, conv_pre[0, 0], point_full)
    first_turn = with_taps(residual, conv_grad, *edges(conv_grad), taps)
    received = lax.ppermute(first_turn, "phase", [(i, i - 1) for i in range(1, phases)])
    arriving = jnp.where(lax.axis_index("phase") == phases - 1, fresh_grad, received)
    near = packed(*[v[None] for v in (arriving, *[along(arriving, -d, False) for d in range(1, SIDE)])])

    back = functools.partial(ff_back, here, 1, own_pre=own_pre, other_pre=other_pre, weights=weights)
    p0, p1, p2, p3 = gathered_back(near, back)
    early = lax.optimization_barrier(sum(v.astype(F32) for v in (p0, along(p1, 1, True), along(p3, 3, True))))
    residual = scattered([early, along(p2, 2, True)], arriving)
    both = jnp.pad(first_turn[None, None], ((0, 1), (0, 0), (0, 0), (0, 0)))
    residual, both = lax.optimization_barrier((residual, both))
    conv_grad = conv_gradient(residual, conv_pre[1, 0], point_full)
    second_turn = with_taps(residual, conv_grad, *edges(conv_grad), taps)
    return lax.dynamic_update_slice(both, second_turn[None, None], (1, 0, 0, 0))


def solution(mesh):
    return jax.shard_map(
        per_device,
        mesh=mesh,
        in_specs=(
            P("phase", None, None),
            P("tensor", None),
            P(None, "phase", None, "tensor"),
            P(None, "phase", "tensor", None),
            P("phase", None, "tensor"),
            P("phase", "tensor", None),
            P("phase", "tensor", None),
            P("phase", None, None),
        ),
        out_specs=P(None, "phase", "tensor", None),
        check_vma=False,
    )
```
